32 devices in a mesh: pipe: 2 (over y), expert: 16 (over z, x, core).
Axes of the slice: x: 2, y: 2, z: 4, core: 2. Of those that a mesh axis runs over, the one named last changes fastest.
Arguments:
- tokens: bfloat16 [2, 2048, 2048], P('pipe', 'expert'), may hold values from -6 to 6
- routes: int32 [2, 2048, 6], P('pipe', 'expert'), may hold values from 0 to 15, all different within a row; in each aligned block of 128 rows (0 to 127, 128 to 255, ..., all dimensions but the last counted through in order) at most 72 rows name the same one
- norm_gain: float32 [2, 2048], P('pipe'), may hold values from 0.1 to 1.9
- router_weight: bfloat16 [2, 2048, 16], P('pipe'), may hold values from -0.125 to 0.125
- w_gate: bfloat16 [2, 16, 2048, 768], P('pipe', 'expert'), may hold values from -0.125 to 0.125
- w_up: bfloat16 [2, 16, 2048, 768], P('pipe', 'expert'), may hold values from -0.125 to 0.125
- w_down: bfloat16 [2, 16, 768, 2048], P('pipe', 'expert'), may hold values from -0.21875 to 0.21875
Outputs:
- received: bfloat16 [2, 2048, 2048], P('pipe', 'expert')
The draws below stay inside these ranges and needn't reach their ends.
Inputs may be any that keep to these rules, and one draw needn't show every extreme that they name: Within each aligned block of 128 tokens of a section (the tokens of one device), the 6 routes of a token name different experts and no expert is named by more than 72 routes; some expert is named by exactly 72 routes in some block; every expert is named somewhere.
All inputs are finite; a program needn't handle non-finite values.
Results may differ from the reference program's by a relative error of at most 0.0039.
Values may be sent and summed in bfloat16 or wider, within the bound.
No kernel may reach another device: no remote copies, remote signals or barrier semaphores. Data moves between devices by JAX's collectives and lax.ppermute only.
A program may use at most 128 MiB of HBM per device.

```python
import math
import jax
import jax.numpy as jnp
import numpy as np
from jax import lax

D = 2048
FF = 768
TOP = 6
TOK_DEV = 128
EXPERTS = 16
SECTIONS = 2
TOKENS = 2048
CAP = 72
N_EXPERT = 16


def levels(rng, dims, cuts, smallest, top_value):
    gain, own = 1.0, jax.random.fold_in(rng, 6)
    for position, blocks in cuts:
        heights = jnp.exp(jax.random.uniform(jax.random.fold_in(own, position), (blocks,), jnp.float32, smallest / len(cuts), top_value / len(cuts)))
        gain = gain * jnp.repeat(heights, dims[position] // blocks).reshape([-1 if axis == position else 1 for axis in range(len(dims))])
    return gain


def routed_block(rng, own, number, rows, amount, top, most, lean):
    order = jax.random.permutation(rng, amount)
    packed, common = shares(amount, rows * top, most, lean, True), shares(amount, rows * top, most, lean, False)
    places = jnp.arange(amount)

    def named(tallies, turn):
        used = int((tallies > 0).sum())
        fixed = max(1, used // 4)
        passed = fixed + (places - fixed + turn * (used - fixed)) % max(1, amount - fixed)
        return jnp.zeros((amount,), jnp.int32).at[order[jnp.where(places < fixed, places, passed)]].set(jnp.asarray(tallies, jnp.int32))

    tallies = jnp.where(number % 4 == 0, named(packed, number // 4), named(common, number - number // 4 - 1))
    mixed = jax.random.permutation(jax.random.fold_in(own, 3), amount)
    giver, sink = mixed[0:amount // 2 * 2:2], mixed[1:amount // 2 * 2:2]
    slack = jnp.minimum(tallies[giver] - 1, most - tallies[sink]) // 2
    slack = jnp.where((giver == order[0]) | (sink == order[0]) | (tallies[sink] == 0), 0, jnp.maximum(slack, 0))
    passed = jax.random.randint(jax.random.fold_in(own, 4), (amount // 2,), 0, 1 << 20) % (slack + 1)
    tallies = tallies.at[giver].add(-passed).at[sink].add(passed)
    items = jnp.searchsorted(jnp.cumsum(tallies), jnp.arange(rows * top), side="right").astype(jnp.int32)
    table = items.reshape(top, rows).T
    table = table[jax.random.permutation(jax.random.fold_in(own, 1), rows)]
    turn = jax.random.randint(jax.random.fold_in(own, 2), (rows, 1), 0, top)
    return jnp.take_along_axis(table, (jnp.arange(top)[None, :] + turn) % top, axis=1)


def shares(amount, total, bound, lean, full):
    loads = [(1 << 20) // math.isqrt(grade ** lean) + 1 for grade in range(1, amount + 1)]
    largest = bound if full else min(bound, max(-(-total // amount), total * loads[0] // sum(loads)))
    least = 1 if total - largest >= amount - 1 else 0
    given, rest = [largest] + [least] * (amount - 1), total - largest - least * (amount - 1)
    while rest > 0:
        candidates = [i for i in range(1, amount) if given[i] < largest] or [i for i in range(1, amount) if given[i] < bound]
        whole, left = sum([loads[i] for i in candidates]), rest
        for i in candidates:
            more = min(bound - given[i], max(1, left * loads[i] // whole), rest)
            given[i] = given[i] + more
            rest = rest - more
    return np.array(given)


def gaussian(key, extent, width, reach, split=(), kind=jnp.bfloat16):
    values = width * jax.random.normal(key, extent, jnp.float32)
    if split:
        values = values * levels(key, extent, split, -0.22, 0.18)
    return jnp.clip(values, -reach, reach).astype(kind)


def setup_inputs(seed: int = 0) -> dict:
    seeds = jax.random.split(jax.random.key(seed), 8)
    tokens = gaussian(seeds[0], (SECTIONS, TOKENS, D), 1.0, 6.0, ((0, 2), (1, 16)))
    routes_keys = jax.random.split(jax.random.fold_in(seeds[1], 1), SECTIONS * TOKENS // TOK_DEV)
    routes_turns = jax.random.permutation(jax.random.fold_in(seeds[1], 3), SECTIONS * TOKENS // TOK_DEV)
    routes = jax.vmap(lambda own, number: routed_block(jax.random.fold_in(seeds[1], 2), own, number, TOK_DEV, EXPERTS, TOP, CAP, 2))(routes_keys, routes_turns).reshape((SECTIONS, TOKENS, TOP))
    norm_gain = jnp.clip(1.0 + 0.18 * jax.random.normal(seeds[2], (SECTIONS, D), jnp.float32), 0.1, 1.9)
    router_weight = gaussian(seeds[3], (SECTIONS, D, EXPERTS), D ** -0.5, 0.125, ((0, 2),))
    w_gate = gaussian(seeds[4], (SECTIONS, EXPERTS, D, FF), D ** -0.5, 0.125, ((0, 2), (1, 16)))
    w_up = gaussian(seeds[5], (SECTIONS, EXPERTS, D, FF), D ** -0.5, 0.125, ((0, 2), (1, 16)))
    w_down = gaussian(seeds[6], (SECTIONS, EXPERTS, FF, D), FF ** -0.5, 0.21875, ((0, 2), (1, 16)))
    return {"tokens": tokens, "routes": routes, "norm_gain": norm_gain, "router_weight": router_weight, "w_gate": w_gate, "w_up": w_up, "w_down": w_down}


def slot_ranks(route_block):
    flat_routes = route_block.reshape(-1)
    hits = (flat_routes[:, None] == jnp.arange(EXPERTS, dtype=jnp.int32)[None, :]).astype(jnp.int32)
    ranks = lax.optimization_barrier(jnp.sum(jnp.cumsum(hits, axis=0) * hits, axis=1)) - 1
    return ranks.reshape(route_block.shape).astype(jnp.int32)

def expert_ffn(slot_block, gate_matrix, up_matrix, down_matrix):
    gate_part = jnp.dot(slot_block, gate_matrix, preferred_element_type=jnp.float32)
    up_part = jnp.dot(slot_block, up_matrix, preferred_element_type=jnp.float32)
    hidden = (jax.nn.silu(gate_part) * up_part).astype(jnp.bfloat16)
    return jnp.dot(hidden, down_matrix, preferred_element_type=jnp.float32).astype(jnp.bfloat16)

def reference(tokens, routes, norm_gain, router_weight, w_gate, w_up, w_down):
    outputs = []
    token_index = jnp.arange(TOKENS, dtype=jnp.int32)
    source = (token_index // TOK_DEV).astype(jnp.int32)
    for section in range(SECTIONS):
        wide_rows = tokens[section].astype(jnp.float32)
        mean_square = lax.optimization_barrier(jnp.mean(wide_rows * wide_rows, axis=-1, keepdims=True))
        normed = (wide_rows * lax.rsqrt(mean_square + 1e-06) * norm_gain[section]).astype(jnp.bfloat16)
        score = jax.nn.sigmoid(jnp.dot(normed, router_weight[section], preferred_element_type=jnp.float32))
        route_now = routes[section]
        picked = jnp.take_along_axis(score, route_now, axis=1)
        gate_values = (picked / lax.optimization_barrier(jnp.sum(picked, axis=1, keepdims=True))).astype(jnp.bfloat16)
        blocks = route_now.reshape(N_EXPERT, TOK_DEV, TOP)
        ranks = jax.vmap(slot_ranks)(blocks).reshape(TOKENS, TOP)
        positions = (source[:, None] * CAP + ranks).astype(jnp.int32)
        owners = jnp.broadcast_to(token_index[:, None], (TOKENS, TOP)).astype(jnp.int32)
        table = jnp.full((EXPERTS, N_EXPERT * CAP), -1, jnp.int32).at[route_now, positions].set(owners)
        valid = table >= 0
        slot_rows = jnp.where(valid[..., None], normed[jnp.maximum(table, 0)], jnp.zeros((), jnp.bfloat16))
        expert_out = lax.map(lambda pack: expert_ffn(pack[0], pack[1], pack[2], pack[3]), (slot_rows, w_gate[section], w_up[section], w_down[section]))
        picked_out = expert_out[route_now, positions]
        moe = jnp.einsum('tk,tkd->td', gate_values.astype(jnp.float32), picked_out.astype(jnp.float32))
        outputs.append((wide_rows + moe).astype(jnp.bfloat16))
    stacked = jnp.stack(outputs)
    return jnp.roll(stacked, 1, axis=0)
```

```python
import jax
import jax.numpy as jnp
from jax import lax
from jax.sharding import PartitionSpec as P


def ring_chips(devices):
    depth = devices // 4
    return [2 * z for z in range(depth)] + [2 * z + 1 for z in reversed(range(depth))]


def ring_pairs(devices, by):
    chips = ring_chips(devices)
    count = len(chips)
    return [
        (2 * chip + core, 2 * chips[(place + by) % count] + core)
        for place, chip in enumerate(chips)
        for core in range(2)
    ]


def round_ring(shard, by):
    return lax.ppermute(shard, "expert", ring_pairs(lax.axis_size("expert"), by))


def across_cores(shard):
    devices = lax.axis_size("expert")
    return lax.ppermute(shard, "expert", [(i, i ^ 1) for i in range(devices)])


def next_section(shard):
    sections = lax.axis_size("pipe")
    return lax.ppermute(shard, "pipe", [(i, (i + 1) % sections) for i in range(sections)])


def gate_table(normed, router, route_local, experts):
    score = jax.nn.sigmoid(jnp.dot(normed, router, preferred_element_type=jnp.float32))
    expert_ids = jnp.arange(experts, dtype=jnp.int32)
    chosen = route_local[..., None] == expert_ids
    picked = jnp.sum(jnp.where(chosen, score[:, None, :], 0.0), axis=-1)
    gate_values = (picked / jnp.sum(picked, axis=1, keepdims=True)).astype(jnp.bfloat16)
    named = jnp.any(chosen, axis=1)
    table = jnp.sum(jnp.where(chosen, gate_values.astype(jnp.float32)[..., None], 0.0), axis=1)
    return jnp.where(named, table, -1.0).astype(jnp.bfloat16).T


def gather_tables(table, chips):
    tables = table[None]
    while tables.shape[0] < chips:
        have = tables.shape[0]
        more = min(have, chips - have)
        tables = jnp.concatenate([tables, round_ring(tables[:more], have)], axis=0)
    return tables


def local(tokens, routes, norm_gain, router_weight, w_gate, w_up, w_down):
    rows = tokens[0]
    route_local = routes[0]
    devices = lax.axis_size("expert")
    chips = devices // 2
    half = chips // 2
    tok_dev, top_count = route_local.shape
    cut = tok_dev // 2
    capacity = 3 * tok_dev * top_count // (2 * devices)
    pair_slots = -(-2 * capacity // 16) * 16
    device = lax.axis_index("expert")
    core = device % 2

    wide_rows = rows.astype(jnp.float32)
    mean_square = jnp.mean(wide_rows * wide_rows, axis=-1, keepdims=True)
    normed = (wide_rows * lax.rsqrt(mean_square + 1e-06) * norm_gain[0]).astype(jnp.bfloat16)
    own = [normed[:cut], normed[cut:]]

    ahead, behind = {0: own}, {0: own}
    for step in range(1, half):
        ahead[step] = [round_ring(part, 1) for part in ahead[step - 1]]
        behind[step] = [round_ring(part, -1) for part in behind[step - 1]]
    far = [round_ring(ahead[half - 1][0], 1), round_ring(behind[half - 1][1], -1)]

    table = gate_table(normed, router_weight[0], route_local, devices)
    tables = gather_tables(table, chips)
    first = lax.dynamic_slice_in_dim(tables, device, 1, axis=1)[:, 0]
    second = lax.dynamic_slice_in_dim(tables, device + 1 - 2 * core, 1, axis=1)[:, 0]
    gates = jnp.stack([first, second], axis=1).astype(jnp.float32)
    named = gates >= 0
    positions = jnp.arange(tok_dev, dtype=jnp.int32)
    earlier = (positions[:, None] < positions[None, :]).astype(jnp.bfloat16)
    ranks = jnp.dot(
        named.astype(jnp.bfloat16).reshape(-1, tok_dev), earlier, preferred_element_type=jnp.float32
    ).astype(jnp.int32).reshape(named.shape)
    order = [[0, half]] + [[k, chips - k] for k in range(1, half)]
    pick = lambda values: jnp.stack(
        [jnp.concatenate([values[a], values[b]], axis=-1) for a, b in order]
    )
    offset = jnp.concatenate(
        [jnp.zeros((tok_dev,), jnp.int32), jnp.full((tok_dev,), capacity, jnp.int32)]
    )
    pair_named, pair_ranks, pair_gates = pick(named), pick(ranks) + offset, pick(gates)
    hits = pair_named[:, :, None, :] & (
        pair_ranks[:, :, None, :] == jnp.arange(pair_slots, dtype=jnp.int32)[:, None]
    )
    selector = hits.astype(jnp.bfloat16)
    weighted = jnp.where(hits, pair_gates[:, :, None, :], 0.0).astype(jnp.bfloat16)

    def pair_rows(k):
        if k == 0:
            return jnp.concatenate(own + far, axis=0)
        return jnp.concatenate(ahead[k] + behind[k], axis=0)

    def experts_out(k):
        block = pair_rows(k)
        taken = jnp.einsum("est,td->esd", selector[k], block, preferred_element_type=jnp.float32)
        taken = taken.astype(jnp.bfloat16)
        slot_rows = jnp.concatenate([taken[0], across_cores(taken[1])], axis=0)
        gate_part = jnp.dot(slot_rows, w_gate[0, 0], preferred_element_type=jnp.float32)
        up_part = jnp.dot(slot_rows, w_up[0, 0], preferred_element_type=jnp.float32)
        hidden = (jax.nn.silu(gate_part) * up_part).astype(jnp.bfloat16)
        out = jnp.dot(hidden, w_down[0, 0], preferred_element_type=jnp.float32).astype(jnp.bfloat16)
        return jnp.stack([out[:pair_slots], across_cores(out[pair_slots:])])

    outs = {k: experts_out(k) for k in list(range(1, half)) + [0]}

    def share(k, begin, count):
        return jnp.einsum(
            "est,esd->td",
            weighted[k][:, :, begin : begin + count],
            outs[k],
            preferred_element_type=jnp.float32,
        )

    bf16 = jnp.bfloat16
    up_low = round_ring(share(0, tok_dev, cut).astype(bf16), 1)
    down_high = round_ring(share(0, tok_dev + cut, cut).astype(bf16), -1)
    up_high = down_low = None
    for k in reversed(range(1, half)):
        before, after = share(k, 0, tok_dev), share(k, tok_dev, tok_dev)
        new_up_high = after[cut:] + (0.0 if up_high is None else up_high.astype(jnp.float32))
        new_down_low = before[:cut] + (0.0 if down_low is None else down_low.astype(jnp.float32))
        new_up_low = after[:cut] + up_low.astype(jnp.float32)
        new_down_high = before[cut:] + down_high.astype(jnp.float32)
        up_high = round_ring(new_up_high.astype(bf16), 1)
        down_low = round_ring(new_down_low.astype(bf16), -1)
        up_low = round_ring(new_up_low.astype(bf16), 1)
        down_high = round_ring(new_down_high.astype(bf16), -1)
    mine = wide_rows + share(0, 0, tok_dev)
    low = mine[:cut] + down_low.astype(jnp.float32) + up_low.astype(jnp.float32)
    high = mine[cut:] + up_high.astype(jnp.float32) + down_high.astype(jnp.float32)
    received = [next_section(low.astype(bf16)), next_section(high.astype(bf16))]
    return jnp.concatenate(received, axis=0)[None]


def solution(mesh):
    return jax.shard_map(
        local,
        mesh=mesh,
        in_specs=(
            P("pipe", "expert", None),
            P("pipe", "expert", None),
            P("pipe", None),
            P("pipe", None, None),
            P("pipe", "expert", None, None),
            P("pipe", "expert", None, None),
            P("pipe", "expert", None, None),
        ),
        out_specs=P("pipe", "expert", None),
        check_vma=False,
    )
```

```python
import functools

import jax
import jax.numpy as jnp
from jax import lax
from jax.experimental import pallas as pl
from jax.experimental.pallas import tpu as pltpu
from jax.sharding import PartitionSpec as P

F32, BF16 = jnp.float32, jnp.bfloat16
SWAPS = 1
ROWS_LAST = (((1,), (1,)), ((), ()))


def ring_chips(devices):
    depth = devices // 4
    return [2 * z for z in range(depth)] + [2 * z + 1 for z in reversed(range(depth))]


def ring_pairs(devices, by):
    chips = ring_chips(devices)
    count = len(chips)
    return [
        (2 * chip + core, 2 * chips[(place + by) % count] + core)
        for place, chip in enumerate(chips)
        for core in range(2)
    ]


def round_ring(shard, by):
    return lax.ppermute(shard, "expert", ring_pairs(lax.axis_size("expert"), by))


def across_cores(shards):
    devices = lax.axis_size("expert")
    return [lax.ppermute(s, "expert", [(i, i ^ 1) for i in range(devices)]) for s in shards]


def next_section(shard):
    sections = lax.axis_size("pipe")
    return lax.ppermute(shard, "pipe", [(i, (i + 1) % sections) for i in range(sections)])


def call(kernel, out_shapes, operands, after=(), grid=None, in_specs=None, out_specs=None,
         scratch=(), megabytes=16, flops=0):
    count = len(operands)

    def body(*refs):
        kernel(*refs[:count], *refs[count + len(after):])

    if in_specs is None:
        in_specs = [pl.BlockSpec(memory_space=pltpu.VMEM)] * count
    if out_specs is None:
        out_specs = [pl.BlockSpec(memory_space=pltpu.VMEM)] * len(out_shapes)
    return pl.pallas_call(
        body,
        out_shape=out_shapes,
        grid=grid or (),
        in_specs=list(in_specs) + [pl.BlockSpec(memory_space=pl.ANY)] * len(after),
        out_specs=out_specs,
        scratch_shapes=list(scratch),
        compiler_params=pltpu.CompilerParams(vmem_limit_bytes=megabytes * 2**20),
        cost_estimate=pl.CostEstimate(flops=int(flops), bytes_accessed=0, transcendentals=0),
    )(*operands, *after)


def prepare_kernel(*refs):
    sources, (low, high), held, arrived = refs[:4], refs[4:6], refs[6:10], refs[10]
    copies = [
        pltpu.make_async_copy(source, target, arrived.at[index])
        for index, (source, target) in enumerate(zip(sources, held))
    ]
    for copy in copies:
        copy.start()
    for copy in copies:
        copy.wait()
    tokens, gain, router, routes = held
    cut, width = high.shape
    experts = router.shape[0]
    wide = tokens[...].astype(F32)
    mean_square = jnp.mean(wide * wide, axis=-1, keepdims=True)
    normed = (wide * lax.rsqrt(mean_square + 1e-06) * gain[...]).astype(BF16)
    low[:, :width] = normed[:cut]
    high[...] = normed[cut:]
    logits = lax.dot_general(router[...], normed, ROWS_LAST, preferred_element_type=F32)
    score = jax.nn.sigmoid(logits)
    ids = lax.broadcasted_iota(jnp.int32, logits.shape, 0)
    named = ids == routes[0]
    for k in range(1, routes.shape[0]):
        named = named | (ids == routes[k])
    total = jnp.sum(jnp.where(named, score, 0.0), axis=0, keepdims=True)
    table = jnp.where(named, (score / total).astype(BF16).astype(F32), -1.0)
    rest = jnp.zeros((cut - experts, logits.shape[1]), F32)
    low[:, width:] = jnp.concatenate([table, rest], axis=0).astype(BF16)


def select_kernel(capacity, blocks, count, names, *refs):
    parts = refs[:count]
    own, info, others = refs[-2 - SWAPS], refs[-1 - SWAPS], refs[-SWAPS:]
    slots, width = own.shape
    tok_dev = parts[0].shape[1] - width
    both = tok_dev * blocks
    firsts = parts[:: len(parts) // blocks]
    table = jnp.concatenate([part[:, width:] for part in firsts], axis=1).astype(F32)
    ids = lax.broadcasted_iota(jnp.int32, table.shape, 0)
    first = jnp.sum(jnp.where(ids == names[0], table, 0.0), axis=0, keepdims=True)
    second = jnp.sum(jnp.where(ids == names[1], table, 0.0), axis=0, keepdims=True)
    line = lax.broadcasted_iota(jnp.int32, (8, both), 0)
    gates = jnp.where(line == 0, first, jnp.where(line == 1, second, -1.0))
    named = gates >= 0
    row = lax.broadcasted_iota(jnp.int32, (both, both), 0)
    column = lax.broadcasted_iota(jnp.int32, (both, both), 1)
    same = (row >= tok_dev) == (column >= tok_dev)
    earlier = jnp.where((row < column) & same, 1.0, 0.0).astype(BF16)
    ranks = jnp.dot(jnp.where(named, 1.0, 0.0).astype(BF16), earlier, preferred_element_type=F32)
    place = lax.broadcasted_iota(jnp.int32, (8, both), 1)
    ranks = jnp.where(place >= tok_dev, ranks + capacity, ranks)
    ranks = jnp.where(named, ranks, -1.0)
    slot = lax.broadcasted_iota(jnp.int32, (slots, both), 0).astype(F32)
    rows = jnp.concatenate([part[:, :width] for part in parts], axis=0)
    hits = jnp.where(slot == ranks[1:2], 1.0, 0.0).astype(BF16)
    span = width // SWAPS
    for index, other in enumerate(others):
        part = rows[:, index * span : (index + 1) * span]
        other[...] = jnp.dot(hits, part, preferred_element_type=F32).astype(BF16)
    hits = jnp.where(slot == ranks[0:1], 1.0, 0.0).astype(BF16)
    own[...] = jnp.dot(hits, rows, preferred_element_type=F32).astype(BF16)
    lines = jnp.where(line < 2, gates, pltpu.roll(ranks, 2, 0))
    spare = jnp.zeros((128 - 8, both), F32)
    info[...] = jnp.concatenate([lines, spare], axis=0).T


def ffn_kernel(tile, own, *refs):
    swapped, (gate, up, down), refs = refs[:SWAPS], refs[SWAPS : SWAPS + 3], refs[SWAPS + 3 :]
    own_out, swapped_outs, (rows, total) = refs[0], refs[1 : 1 + SWAPS], refs[1 + SWAPS :]
    slots, span = swapped[0].shape
    rows[:slots] = own[...]
    for index, part in enumerate(swapped):
        rows[slots:, index * span : (index + 1) * span] = part[...]

    def terms(step):
        columns = pl.ds(pl.multiple_of(step * tile, tile), tile)
        gate_part = jnp.dot(rows[...], gate[:, columns], preferred_element_type=F32)
        up_part = jnp.dot(rows[...], up[:, columns], preferred_element_type=F32)
        hidden = (gate_part / (1.0 + jnp.exp(-gate_part)) * up_part).astype(BF16)
        return jnp.dot(hidden, down[columns, :], preferred_element_type=F32)

    steps = gate.shape[1] // tile
    total[...] = terms(0)

    @pl.loop(1, steps - 1)
    def _(step):
        total[...] += terms(step)

    result = total[...] + terms(steps - 1)
    own_out[...] = result[:slots].astype(BF16)
    for index, target in enumerate(swapped_outs):
        target[...] = result[slots:, index * span : (index + 1) * span].astype(BF16)


def weights_of(info, begin, count, slots):
    block = info[begin : begin + count, :]
    slot = lax.broadcasted_iota(jnp.int32, (count, slots), 1).astype(F32)
    return [
        jnp.where(slot == block[:, 2 + e : 3 + e], block[:, e : e + 1], 0.0).astype(BF16)
        for e in range(2)
    ]


def expert_sum(begins, count, info, own_out, *other_out):
    slots = own_out.shape[0]
    weights = [weights_of(info, begin, count, slots) for begin in begins]
    own_weights = jnp.concatenate([w[0] for w in weights], axis=0)
    other_weights = jnp.concatenate([w[1] for w in weights], axis=0)
    return jnp.dot(own_weights, own_out[...], preferred_element_type=F32) + jnp.concatenate(
        [jnp.dot(other_weights, o[...], preferred_element_type=F32) for o in other_out], axis=1
    )


def own_kernel(*refs):
    outs, (tokens, low, high) = refs[:-3], refs[-3:]
    cut = low.shape[0]
    value = expert_sum((0,), 2 * cut, *outs) + tokens[...].astype(F32)
    low[...] = value[:cut]
    high[...] = value[cut:]


def final_kernel(mine, up, up_last, down, down_last, target):
    quarter = up_last.shape[0]
    for here, first, second in ((0, up_last, down), (quarter, up, down_last)):
        begin = quarter if first is up else 0
        value = mine[here : here + quarter, :] + first[begin : begin + quarter, :].astype(F32)
        begin = quarter if second is down else 0
        value += second[begin : begin + quarter, :].astype(F32)
        target[here : here + quarter, :] = value.astype(BF16)


def hop_kernel(begins, sums, *refs):
    size = 2 + SWAPS
    count = refs[-1].shape[0] // len(begins)
    came, targets = refs[size * len(begins) : -2], refs[-2:]
    for place, pair in enumerate(begins):
        part = expert_sum(pair, count, *refs[size * place : size * (place + 1)])
        for index, target in enumerate(targets):
            value = part[index * count : (index + 1) * count]
            here = pl.ds(place * count, count)
            if sums:
                value += came[index][here, :].astype(F32)
            target[here, :] = value.astype(target.dtype)


def shape(rows, columns, dtype=BF16):
    return jax.ShapeDtypeStruct((rows, columns), dtype)


def local(tokens, routes, norm_gain, router_weight, w_gate, w_up, w_down):
    rows = tokens[0]
    devices = lax.axis_size("expert")
    chips = devices // 2
    half = chips // 2
    tok_dev, top_count = routes.shape[1:]
    width = rows.shape[1]
    cut, quarter = tok_dev // 2, tok_dev // 4
    capacity = 3 * tok_dev * top_count // (2 * devices)
    device = lax.axis_index("expert")
    names = jnp.stack([device, device ^ 1]).astype(jnp.int32)
    gate, up, down = w_gate[0, 0], w_up[0, 0], w_down[0, 0]
    hidden = gate.shape[1]
    tile = 256 if hidden % 256 == 0 else hidden

    sources = [rows, norm_gain, router_weight[0].T, jnp.transpose(routes, (2, 0, 1))]
    own = call(
        prepare_kernel,
        [shape(cut, width + tok_dev), shape(cut, width)],
        sources,
        in_specs=[pl.BlockSpec(memory_space=pltpu.HBM)] * len(sources),
        scratch=[pltpu.VMEM(a.shape, a.dtype) for a in sources]
        + [pltpu.SemaphoreType.DMA((len(sources),))],
    )

    def select(parts, blocks, after, held=()):
        slots = -(-blocks * capacity // 16) * 16
        return call(
            functools.partial(select_kernel, capacity, blocks, len(parts)),
            [shape(slots, width), shape(blocks * tok_dev, 128, F32)]
            + [shape(slots, width // SWAPS)] * SWAPS,
            [names, *parts, *held],
            after,
            in_specs=[pl.BlockSpec(memory_space=pltpu.SMEM)]
            + [pl.BlockSpec(memory_space=pltpu.VMEM)] * (len(parts) + len(held)),
            flops=2e8 * blocks,
        )

    def ffn(own_rows, swapped_rows, after):
        slots = own_rows.shape[0]
        return call(
            functools.partial(ffn_kernel, tile),
            [shape(slots, width)] + [shape(slots, width // SWAPS)] * SWAPS,
            [own_rows, *swapped_rows, gate, up, down],
            after,
            scratch=[pltpu.VMEM((2 * slots, width), BF16), pltpu.VMEM((2 * slots, width), F32)],
            megabytes=24,
            flops=6e7 * slots,
        )

    def hop(number, high, came, after):
        far_group, near_group = half + 1 - number, half - number
        base = cut if high else 0

        def begins(group, first):
            offset = 0 if group == half else tok_dev
            return (base + first + offset, base + quarter - first)

        groups = [(far_group, begins(far_group, 0))]
        if near_group:
            groups.append((near_group, begins(near_group, quarter)))
        return call(
            functools.partial(hop_kernel, tuple(b for _, b in groups), bool(came)),
            [shape(quarter * len(groups), width)] * 2,
            [array for group, _ in groups for array in outs[group]] + list(came),
            after,
        )

    def send(pair):
        return [round_ring(pair[0], 1), round_ring(pair[1], -1)]

    ahead, behind = {0: own}, {0: own}
    for step in range(1, half):
        ahead[step] = [round_ring(part, 1) for part in ahead[step - 1]]
        behind[step] = [round_ring(part, -1) for part in behind[step - 1]]
    far = []
    for index in range(2):
        far.append(round_ring(ahead[half - 1][index][:quarter], 1))
        far.append(round_ring(behind[half - 1][index][quarter:], -1))

    parts = {k: ahead[k] + behind[k] for k in range(1, half)}
    parts[0], parts[half] = own, far
    picked, outs = {}, {}

    def run_select(k, *after):
        own_rows, info, *other_rows = select(
            parts[k], 1 if k in (0, half) else 2, after, [gate, up, down] if k == 0 else []
        )
        picked[k] = (own_rows, across_cores(other_rows), info)

    def run_ffn(k, *after):
        own_rows, swapped_rows, info = picked[k]
        own_out, *swapped_out = ffn(own_rows, swapped_rows, after)
        outs[k] = (info, own_out, *across_cores(swapped_out))

    def selected(k):
        return picked[k][2]

    def worked(k):
        return outs[k][1]

    run_select(0)
    run_ffn(0)
    for k in range(1, half):
        run_select(k)
    for k in range(1, half - 1):
        run_ffn(k, worked(k - 1))
    run_select(half, worked(half - 2))
    run_ffn(half - 1, selected(half))
    run_ffn(half, worked(half - 1))

    low_sums, high_sums, mine, last, kept = (), (), None, (), {}
    for number in range(1, half + 1):
        sums = hop(number, False, low_sums, last)
        last = (sums[0],)
        low_sums = send(sums)
        sums = hop(number, True, high_sums, last)
        last = (sums[0],)
        high_sums = send(sums)
        kept[number] = (low_sums, high_sums)
        if mine is None:
            mine = call(own_kernel, [shape(cut, width, F32)] * 2, [*outs[0], rows], last)
            last = (mine[0],)
    received = []
    for index in range(2):
        (up_last, down_last), (up, down) = kept[half][index], kept[half - 1][index]
        total = call(
            final_kernel, [shape(cut, width)], [mine[index], up, up_last, down, down_last]
        )
        received.append(next_section(total[0]))
    return jnp.concatenate(received, axis=0)[None]


def solution(mesh):
    return jax.shard_map(
        local,
        mesh=mesh,
        in_specs=(
            P("pipe", "expert", None),
            P("pipe", "expert", None),
            P("pipe", None),
            P("pipe", None, None),
            P("pipe", "expert", None, None),
            P("pipe", "expert", None, None),
            P("pipe", "expert", None, None),
        ),
        out_specs=P("pipe", "expert", None),
        check_vma=False,
    )
```

```python
import functools

import jax
import jax.numpy as jnp
from jax import lax
from jax.experimental import pallas as pl
from jax.experimental.pallas import tpu as pltpu
from jax.sharding import PartitionSpec as P

F32, BF16 = jnp.float32, jnp.bfloat16
SWAPS = 1
ROWS_LAST = (((1,), (1,)), ((), ()))


def ring_chips(devices):
    depth = devices // 4
    return [2 * z for z in range(depth)] + [2 * z + 1 for z in reversed(range(depth))]


def ring_pairs(devices, by):
    chips = ring_chips(devices)
    count = len(chips)
    return [
        (2 * chip + core, 2 * chips[(place + by) % count] + core)
        for place, chip in enumerate(chips)
        for core in range(2)
    ]


def round_ring(shard, by):
    return lax.ppermute(shard, "expert", ring_pairs(lax.axis_size("expert"), by))


def across_cores(shards):
    devices = lax.axis_size("expert")
    return [lax.ppermute(s, "expert", [(i, i ^ 1) for i in range(devices)]) for s in shards]


def next_section(shard):
    sections = lax.axis_size("pipe")
    return lax.ppermute(shard, "pipe", [(i, (i + 1) % sections) for i in range(sections)])


def call(kernel, out_shapes, operands, after=(), grid=None, in_specs=None, out_specs=None,
         scratch=(), megabytes=16, flops=0, name=None):
    count = len(operands)

    def body(*refs):
        kernel(*refs[:count], *refs[count + len(after):])

    if in_specs is None:
        in_specs = [pl.BlockSpec(memory_space=pltpu.VMEM)] * count
    if out_specs is None:
        out_specs = [pl.BlockSpec(memory_space=pltpu.VMEM)] * len(out_shapes)
    return pl.pallas_call(
        body,
        name=name,
        out_shape=out_shapes,
        grid=grid or (),
        in_specs=list(in_specs) + [pl.BlockSpec(memory_space=pl.ANY)] * len(after),
        out_specs=out_specs,
        scratch_shapes=list(scratch),
        compiler_params=pltpu.CompilerParams(vmem_limit_bytes=megabytes * 2**20),
        cost_estimate=pl.CostEstimate(flops=int(flops), bytes_accessed=0, transcendentals=0),
    )(*operands, *after)


def prepare_kernel(*refs):
    sources, (low, high), held, arrived = refs[:4], refs[4:6], refs[6:10], refs[10]
    copies = [
        pltpu.make_async_copy(source, target, arrived.at[index])
        for index, (source, target) in enumerate(zip(sources, held))
    ]
    for copy in copies:
        copy.start()
    for copy in copies:
        copy.wait()
    tokens, gain, router, routes = held
    cut, width = low.shape[0], tokens.shape[1]
    experts = router.shape[0]
    wide = tokens[...].astype(F32)
    mean_square = jnp.mean(wide * wide, axis=-1, keepdims=True)
    normed = (wide * lax.rsqrt(mean_square + 1e-06) * gain[...]).astype(BF16)
    low[:, :width] = normed[:cut]
    high[...] = normed[cut:]
    logits = lax.dot_general(router[...], normed, ROWS_LAST, preferred_element_type=F32)
    score = jax.nn.sigmoid(logits)
    ids = lax.broadcasted_iota(jnp.int32, logits.shape, 0)
    named = ids == routes[0]
    for k in range(1, routes.shape[0]):
        named = named | (ids == routes[k])
    total = jnp.sum(jnp.where(named, score, 0.0), axis=0, keepdims=True)
    table = jnp.where(named, (score / total).astype(BF16).astype(F32), -1.0)
    rest = jnp.zeros((cut - experts, logits.shape[1]), F32)
    low[:, width:] = jnp.concatenate([table, rest], axis=0).astype(BF16)


def select_kernel(capacity, blocks, count, names, *refs):
    parts = refs[:count]
    own, info, others = refs[-2 - SWAPS], refs[-1 - SWAPS], refs[-SWAPS:]
    slots, width = own.shape
    tok_dev = parts[0].shape[1] - width
    both = tok_dev * blocks
    firsts = parts[:: len(parts) // blocks]
    table = jnp.concatenate([part[:, width:] for part in firsts], axis=1).astype(F32)
    ids = lax.broadcasted_iota(jnp.int32, table.shape, 0)
    first = jnp.sum(jnp.where(ids == names[0], table, 0.0), axis=0, keepdims=True)
    second = jnp.sum(jnp.where(ids == names[1], table, 0.0), axis=0, keepdims=True)
    line = lax.broadcasted_iota(jnp.int32, (8, both), 0)
    gates = jnp.where(line == 0, first, jnp.where(line == 1, second, -1.0))
    named = gates >= 0
    row = lax.broadcasted_iota(jnp.int32, (both, both), 0)
    column = lax.broadcasted_iota(jnp.int32, (both, both), 1)
    same = (row >= tok_dev) == (column >= tok_dev)
    earlier = jnp.where((row < column) & same, 1.0, 0.0).astype(BF16)
    ranks = jnp.dot(jnp.where(named, 1.0, 0.0).astype(BF16), earlier, preferred_element_type=F32)
    place = lax.broadcasted_iota(jnp.int32, (8, both), 1)
    ranks = jnp.where(place >= tok_dev, ranks + capacity, ranks)
    ranks = jnp.where(named, ranks, -1.0)
    slot = lax.broadcasted_iota(jnp.int32, (slots, both), 0).astype(F32)
    rows = jnp.concatenate([part[:, :width] for part in parts], axis=0)
    hits = jnp.where(slot == ranks[1:2], 1.0, 0.0).astype(BF16)
    span = width // SWAPS
    for index, other in enumerate(others):
        part = rows[:, index * span : (index + 1) * span]
        other[...] = jnp.dot(hits, part, preferred_element_type=F32).astype(BF16)
    hits = jnp.where(slot == ranks[0:1], 1.0, 0.0).astype(BF16)
    own[...] = jnp.dot(hits, rows, preferred_element_type=F32).astype(BF16)
    lines = jnp.where(line < 2, gates, pltpu.roll(ranks, 2, 0))
    spare = jnp.zeros((128 - 8, both), F32)
    info[...] = jnp.concatenate([lines, spare], axis=0).T


def ffn_kernel(tile, own, *refs):
    swapped, (gate, up, down), refs = refs[:SWAPS], refs[SWAPS : SWAPS + 3], refs[SWAPS + 3 :]
    own_out, swapped_outs, (rows, total) = refs[0], refs[1 : 1 + SWAPS], refs[1 + SWAPS :]
    slots, span = swapped[0].shape
    rows[:slots] = own[...]
    for index, part in enumerate(swapped):
        rows[slots:, index * span : (index + 1) * span] = part[...]

    def terms(step):
        columns = pl.ds(pl.multiple_of(step * tile, tile), tile)
        gate_part = jnp.dot(rows[...], gate[:, columns], preferred_element_type=F32)
        up_part = jnp.dot(rows[...], up[:, columns], preferred_element_type=F32)
        hidden = (gate_part / (1.0 + jnp.exp(-gate_part)) * up_part).astype(BF16)
        return jnp.dot(hidden, down[columns, :], preferred_element_type=F32)

    steps = gate.shape[1] // tile
    total[...] = terms(0)

    @pl.loop(1, steps - 1)
    def _(step):
        total[...] += terms(step)

    result = total[...] + terms(steps - 1)
    own_out[...] = result[:slots].astype(BF16)
    for index, target in enumerate(swapped_outs):
        target[...] = result[slots:, index * span : (index + 1) * span].astype(BF16)


def weights_of(info, begin, count, slots):
    block = info[begin : begin + count, :]
    slot = lax.broadcasted_iota(jnp.int32, (count, slots), 1).astype(F32)
    return [
        jnp.where(slot == block[:, 2 + e : 3 + e], block[:, e : e + 1], 0.0).astype(BF16)
        for e in range(2)
    ]


def expert_sum(begins, count, info, own_out, *other_out):
    slots = own_out.shape[0]
    weights = [weights_of(info, begin, count, slots) for begin in begins]
    own_weights = jnp.concatenate([w[0] for w in weights], axis=0)
    other_weights = jnp.concatenate([w[1] for w in weights], axis=0)
    return jnp.dot(own_weights, own_out[...], preferred_element_type=F32) + jnp.concatenate(
        [jnp.dot(other_weights, o[...], preferred_element_type=F32) for o in other_out], axis=1
    )


def own_kernel(*refs):
    outs, (tokens, low, high) = refs[:-3], refs[-3:]
    cut = low.shape[0]
    value = expert_sum((0,), 2 * cut, *outs) + tokens[...].astype(F32)
    low[...] = value[:cut]
    high[...] = value[cut:]


def tie(array, *tokens):
    return lax.optimization_barrier((array, *tokens))[0]


def final_kernel(mine, up, up_last, down, down_last, target):
    quarter = up_last.shape[0]
    for here, first, second in ((0, up_last, down), (quarter, up, down_last)):
        begin = quarter if first is up else 0
        value = mine[here : here + quarter, :] + first[begin : begin + quarter, :].astype(F32)
        begin = quarter if second is down else 0
        value += second[begin : begin + quarter, :].astype(F32)
        target[here : here + quarter, :] = value.astype(BF16)


def hop_kernel(begins, sums, *refs):
    size = 2 + SWAPS
    count = refs[-1].shape[0] // len(begins)
    came, targets = refs[size * len(begins) : -2], refs[-2:]
    for place, pair in enumerate(begins):
        part = expert_sum(pair, count, *refs[size * place : size * (place + 1)])
        for index, target in enumerate(targets):
            value = part[index * count : (index + 1) * count]
            here = pl.ds(place * count, count)
            if sums:
                value += came[index][here, :].astype(F32)
            target[here, :] = value.astype(target.dtype)


def shape(rows, columns, dtype=BF16):
    return jax.ShapeDtypeStruct((rows, columns), dtype)


def local(tokens, routes, norm_gain, router_weight, w_gate, w_up, w_down):
    rows = tokens[0]
    devices = lax.axis_size("expert")
    chips = devices // 2
    half = chips // 2
    tok_dev, top_count = routes.shape[1:]
    width = rows.shape[1]
    cut, quarter = tok_dev // 2, tok_dev // 4
    capacity = 3 * tok_dev * top_count // (2 * devices)
    device = lax.axis_index("expert")
    names = jnp.stack([device, device ^ 1]).astype(jnp.int32)
    gate, up, down = w_gate[0, 0], w_up[0, 0], w_down[0, 0]
    hidden = gate.shape[1]
    tile = 256 if hidden % 256 == 0 else hidden

    sources = [rows, norm_gain, router_weight[0].T, jnp.transpose(routes, (2, 0, 1))]
    own = call(
        prepare_kernel,
        [shape(cut, width + tok_dev), shape(cut, width)],
        sources,
        name="prepare",
        in_specs=[pl.BlockSpec(memory_space=pltpu.HBM)] * len(sources),
        scratch=[pltpu.VMEM(a.shape, a.dtype) for a in sources]
        + [pltpu.SemaphoreType.DMA((len(sources),))],
        megabytes=56,
    )

    def select(parts, blocks, after, held=()):
        slots = -(-blocks * capacity // 16) * 16
        return call(
            functools.partial(select_kernel, capacity, blocks, len(parts)),
            [shape(slots, width), shape(blocks * tok_dev, 128, F32)]
            + [shape(slots, width // SWAPS)] * SWAPS,
            [names, *parts, *held],
            after,
            in_specs=[pl.BlockSpec(memory_space=pltpu.SMEM)]
            + [pl.BlockSpec(memory_space=pltpu.VMEM)] * (len(parts) + len(held)),
            flops=2e8 * blocks,
            name=f"select{blocks}",
        )

    def ffn(own_rows, swapped_rows, after):
        slots = own_rows.shape[0]
        return call(
            functools.partial(ffn_kernel, tile),
            [shape(slots, width)] + [shape(slots, width // SWAPS)] * SWAPS,
            [own_rows, *swapped_rows, gate, up, down],
            after,
            scratch=[pltpu.VMEM((2 * slots, width), BF16), pltpu.VMEM((2 * slots, width), F32)],
            megabytes=24,
            flops=6e7 * slots,
            name=f"ffn{1 + (slots > 100)}",
        )

    def hop(number, high, came, after):
        far_group, near_group = half + 1 - number, half - number
        base = cut if high else 0

        def begins(group, first):
            offset = 0 if group == half else tok_dev
            return (base + first + offset, base + quarter - first)

        groups = [(far_group, begins(far_group, 0))]
        if near_group:
            groups.append((near_group, begins(near_group, quarter)))
        return call(
            functools.partial(hop_kernel, tuple(b for _, b in groups), bool(came)),
            [shape(quarter * len(groups), width)] * 2,
            [array for group, _ in groups for array in outs[group]] + list(came),
            after,
            name="hop",
        )

    def send(pair):
        return [round_ring(pair[0], 1), round_ring(pair[1], -1)]

    picked, outs, parts = {}, {}, {0: own}

    def run_select(k, *after):
        own_rows, info, *other_rows = select(
            parts[k], 1 if k in (0, half) else 2, after, [gate, up, down] if k == 0 else []
        )
        picked[k] = (own_rows, across_cores(other_rows), info)

    def run_ffn(k, *after):
        own_rows, swapped_rows, info = picked[k]
        own_out, *swapped_out = ffn(own_rows, swapped_rows, after)
        outs[k] = (info, own_out, *across_cores(swapped_out))

    def selected(k):
        return picked[k][2]

    def worked(k):
        return outs[k][1]

    run_select(0)
    run_ffn(0)
    ahead, behind = list(own), list(own)
    for k in range(1, half):
        ahead = [round_ring(part, 1) for part in ahead]
        behind = [round_ring(part, -1) for part in behind]
        parts[k] = ahead + behind
        run_select(k, *(picked[k - 1][1] if k > 1 else []))
        if k < half - 1:
            run_ffn(k, worked(k - 1))
    early = (worked(half - 3), *picked[half - 2][1])
    ahead[0], behind[0] = tie(ahead[0], *early), tie(behind[0], *early)
    far = []
    for index in range(2):
        far.append(round_ring(ahead[index][:quarter], 1))
        far.append(round_ring(behind[index][quarter:], -1))
    parts[half] = far
    run_select(half, worked(half - 2))
    run_ffn(half - 1, selected(half))
    run_ffn(half, worked(half - 1))

    low_sums, high_sums, mine, last, kept = (), (), None, (), {}
    for number in range(1, half + 1):
        sums = hop(number, False, low_sums, last)
        last = (sums[0],)
        low_sums = send(sums)
        sums = hop(number, True, high_sums, last)
        last = (sums[0],)
        high_sums = send(sums)
        kept[number] = (low_sums, high_sums)
        if mine is None:
            mine = call(own_kernel, [shape(cut, width, F32)] * 2, [*outs[0], rows], last, name="mine")
            last = (mine[0],)
    received = []
    for index in range(2):
        (up_last, down_last), (up, down) = kept[half][index], kept[half - 1][index]
        total = call(
            final_kernel, [shape(cut, width)], [mine[index], up, up_last, down, down_last], name="final"
        )
        received.append(next_section(total[0]))
    return jnp.concatenate(received, axis=0)[None]


def solution(mesh):
    return jax.shard_map(
        local,
        mesh=mesh,
        in_specs=(
            P("pipe", "expert", None),
            P("pipe", "expert", None),
            P("pipe", None),
            P("pipe", None, None),
            P("pipe", "expert", None, None),
            P("pipe", "expert", None, None),
            P("pipe", "expert", None, None),
        ),
        out_specs=P("pipe", "expert", None),
        check_vma=False,
    )
```

```python
import functools

import jax
import jax.numpy as jnp
from jax import lax
from jax.experimental import pallas as pl
from jax.experimental.pallas import tpu as pltpu
from jax.sharding import PartitionSpec as P

F32, BF16 = jnp.float32, jnp.bfloat16
SWAPS = 1
ROWS_LAST = (((1,), (1,)), ((), ()))


def ring_chips(devices):
    depth = devices // 4
    return [2 * z for z in range(depth)] + [2 * z + 1 for z in reversed(range(depth))]


def ring_pairs(devices, by):
    chips = ring_chips(devices)
    count = len(chips)
    return [
        (2 * chip + core, 2 * chips[(place + by) % count] + core)
        for place, chip in enumerate(chips)
        for core in range(2)
    ]


def round_ring(shard, by):
    return lax.ppermute(shard, "expert", ring_pairs(lax.axis_size("expert"), by))


def across_cores(shards):
    devices = lax.axis_size("expert")
    return [lax.ppermute(s, "expert", [(i, i ^ 1) for i in range(devices)]) for s in shards]


def next_section(shard):
    sections = lax.axis_size("pipe")
    return lax.ppermute(shard, "pipe", [(i, (i + 1) % sections) for i in range(sections)])


def call(kernel, out_shapes, operands, after=(), grid=None, in_specs=None, out_specs=None,
         scratch=(), megabytes=16, flops=0, name=None):
    count = len(operands)

    def body(*refs):
        kernel(*refs[:count], *refs[count + len(after):])

    if in_specs is None:
        in_specs = [pl.BlockSpec(memory_space=pltpu.VMEM)] * count
    if out_specs is None:
        out_specs = [pl.BlockSpec(memory_space=pltpu.VMEM)] * len(out_shapes)
    return pl.pallas_call(
        body,
        name=name,
        out_shape=out_shapes,
        grid=grid or (),
        in_specs=list(in_specs) + [pl.BlockSpec(memory_space=pl.ANY)] * len(after),
        out_specs=out_specs,
        scratch_shapes=list(scratch),
        compiler_params=pltpu.CompilerParams(vmem_limit_bytes=megabytes * 2**20),
        cost_estimate=pl.CostEstimate(flops=int(flops), bytes_accessed=0, transcendentals=0),
    )(*operands, *after)


def prepare_kernel(*refs):
    sources, (low, high), held, arrived = refs[:4], refs[4:6], refs[6:10], refs[10]
    copies = [
        pltpu.make_async_copy(source, target, arrived.at[index])
        for index, (source, target) in enumerate(zip(sources, held))
    ]
    for copy in copies:
        copy.start()
    for copy in copies:
        copy.wait()
    tokens, gain, router, routes = held
    cut, width = low.shape[0], tokens.shape[1]
    experts = router.shape[0]
    wide = tokens[...].astype(F32)
    mean_square = jnp.mean(wide * wide, axis=-1, keepdims=True)
    normed = (wide * lax.rsqrt(mean_square + 1e-06) * gain[...]).astype(BF16)
    low[:, :width] = normed[:cut]
    high[...] = normed[cut:]
    logits = lax.dot_general(router[...], normed, ROWS_LAST, preferred_element_type=F32)
    score = jax.nn.sigmoid(logits)
    ids = lax.broadcasted_iota(jnp.int32, logits.shape, 0)
    named = ids == routes[0]
    for k in range(1, routes.shape[0]):
        named = named | (ids == routes[k])
    total = jnp.sum(jnp.where(named, score, 0.0), axis=0, keepdims=True)
    table = jnp.where(named, (score / total).astype(BF16).astype(F32), -1.0)
    rest = jnp.zeros((cut - experts, logits.shape[1]), F32)
    low[:, width:] = jnp.concatenate([table, rest], axis=0).astype(BF16)


def select_kernel(capacity, blocks, count, names, *refs):
    parts = refs[:count]
    own, info, others = refs[-2 - SWAPS], refs[-1 - SWAPS], refs[-SWAPS:]
    slots, width = own.shape
    tok_dev = parts[0].shape[1] - width
    both = tok_dev * blocks
    firsts = parts[:: len(parts) // blocks]
    table = jnp.concatenate([part[:, width:] for part in firsts], axis=1).astype(F32)
    ids = lax.broadcasted_iota(jnp.int32, table.shape, 0)
    first = jnp.sum(jnp.where(ids == names[0], table, 0.0), axis=0, keepdims=True)
    second = jnp.sum(jnp.where(ids == names[1], table, 0.0), axis=0, keepdims=True)
    line = lax.broadcasted_iota(jnp.int32, (8, both), 0)
    gates = jnp.where(line == 0, first, jnp.where(line == 1, second, -1.0))
    named = gates >= 0
    row = lax.broadcasted_iota(jnp.int32, (both, both), 0)
    column = lax.broadcasted_iota(jnp.int32, (both, both), 1)
    same = (row >= tok_dev) == (column >= tok_dev)
    earlier = jnp.where((row < column) & same, 1.0, 0.0).astype(BF16)
    ranks = jnp.dot(jnp.where(named, 1.0, 0.0).astype(BF16), earlier, preferred_element_type=F32)
    place = lax.broadcasted_iota(jnp.int32, (8, both), 1)
    ranks = jnp.where(place >= tok_dev, ranks + capacity, ranks)
    ranks = jnp.where(named, ranks, -1.0)
    slot = lax.broadcasted_iota(jnp.int32, (slots, both), 0).astype(F32)
    rows = jnp.concatenate([part[:, :width] for part in parts], axis=0)
    hits = jnp.where(slot == ranks[1:2], 1.0, 0.0).astype(BF16)
    span = width // SWAPS
    for index, other in enumerate(others):
        part = rows[:, index * span : (index + 1) * span]
        other[...] = jnp.dot(hits, part, preferred_element_type=F32).astype(BF16)
    hits = jnp.where(slot == ranks[0:1], 1.0, 0.0).astype(BF16)
    own[...] = jnp.dot(hits, rows, preferred_element_type=F32).astype(BF16)
    lines = jnp.where(line < 2, gates, pltpu.roll(ranks, 2, 0))
    spare = jnp.zeros((128 - 8, both), F32)
    info[...] = jnp.concatenate([lines, spare], axis=0).T


def ffn_kernel(own, *refs):
    swapped, (gate, up, down), refs = refs[:SWAPS], refs[SWAPS : SWAPS + 3], refs[SWAPS + 3 :]
    own_out, swapped_outs, rows = refs[0], refs[1 : 1 + SWAPS], refs[1 + SWAPS]
    slots, span = swapped[0].shape
    rows[:slots] = own[...]
    for index, part in enumerate(swapped):
        rows[slots:, index * span : (index + 1) * span] = part[...]

    gate_part = jnp.dot(rows[...], gate[...], preferred_element_type=F32)
    up_part = jnp.dot(rows[...], up[...], preferred_element_type=F32)
    hidden = (gate_part / (1.0 + jnp.exp(-gate_part)) * up_part).astype(BF16)
    result = jnp.dot(hidden, down[...], preferred_element_type=F32)
    own_out[...] = result[:slots].astype(BF16)
    for index, target in enumerate(swapped_outs):
        target[...] = result[slots:, index * span : (index + 1) * span].astype(BF16)


def weights_of(info, begin, count, slots):
    block = info[begin : begin + count, :]
    slot = lax.broadcasted_iota(jnp.int32, (count, slots), 1).astype(F32)
    return [
        jnp.where(slot == block[:, 2 + e : 3 + e], block[:, e : e + 1], 0.0).astype(BF16)
        for e in range(2)
    ]


def expert_sum(begins, count, info, own_out, *other_out):
    slots = own_out.shape[0]
    weights = [weights_of(info, begin, count, slots) for begin in begins]
    own_weights = jnp.concatenate([w[0] for w in weights], axis=0)
    other_weights = jnp.concatenate([w[1] for w in weights], axis=0)
    return jnp.dot(own_weights, own_out[...], preferred_element_type=F32) + jnp.concatenate(
        [jnp.dot(other_weights, o[...], preferred_element_type=F32) for o in other_out], axis=1
    )


def own_kernel(*refs):
    outs, (tokens, low, high) = refs[:-3], refs[-3:]
    cut = low.shape[0]
    value = expert_sum((0,), 2 * cut, *outs) + tokens[...].astype(F32)
    low[...] = value[:cut]
    high[...] = value[cut:]


def tie(array, *tokens):
    return lax.optimization_barrier((array, *tokens))[0]


def final_kernel(mine, up, up_last, down, down_last, target):
    quarter = up_last.shape[0]
    for here, first, second in ((0, up_last, down), (quarter, up, down_last)):
        begin = quarter if first is up else 0
        value = mine[here : here + quarter, :] + first[begin : begin + quarter, :].astype(F32)
        begin = quarter if second is down else 0
        value += second[begin : begin + quarter, :].astype(F32)
        target[here : here + quarter, :] = value.astype(BF16)


def hop_kernel(begins, sums, *refs):
    size = 2 + SWAPS
    count = refs[-1].shape[0] // len(begins)
    came, targets = refs[size * len(begins) : -2], refs[-2:]
    for place, pair in enumerate(begins):
        part = expert_sum(pair, count, *refs[size * place : size * (place + 1)])
        for index, target in enumerate(targets):
            value = part[index * count : (index + 1) * count]
            here = pl.ds(place * count, count)
            if sums:
                value += came[index][here, :].astype(F32)
            target[here, :] = value.astype(target.dtype)


def shape(rows, columns, dtype=BF16):
    return jax.ShapeDtypeStruct((rows, columns), dtype)


def local(tokens, routes, norm_gain, router_weight, w_gate, w_up, w_down):
    rows = tokens[0]
    devices = lax.axis_size("expert")
    chips = devices // 2
    half = chips // 2
    tok_dev, top_count = routes.shape[1:]
    width = rows.shape[1]
    cut, quarter = tok_dev // 2, tok_dev // 4
    capacity = 3 * tok_dev * top_count // (2 * devices)
    device = lax.axis_index("expert")
    names = jnp.stack([device, device ^ 1]).astype(jnp.int32)
    gate, up, down = w_gate[0, 0], w_up[0, 0], w_down[0, 0]

    sources = [rows, norm_gain, router_weight[0].T, jnp.transpose(routes, (2, 0, 1))]
    own = call(
        prepare_kernel,
        [shape(cut, width + tok_dev), shape(cut, width)],
        sources,
        name="prepare",
        in_specs=[pl.BlockSpec(memory_space=pltpu.HBM)] * len(sources),
        scratch=[pltpu.VMEM(a.shape, a.dtype) for a in sources]
        + [pltpu.SemaphoreType.DMA((len(sources),))],
        megabytes=56,
    )

    def select(parts, blocks, after, held=()):
        slots = -(-blocks * capacity // 16) * 16
        return call(
            functools.partial(select_kernel, capacity, blocks, len(parts)),
            [shape(slots, width), shape(blocks * tok_dev, 128, F32)]
            + [shape(slots, width // SWAPS)] * SWAPS,
            [names, *parts, *held],
            after,
            in_specs=[pl.BlockSpec(memory_space=pltpu.SMEM)]
            + [pl.BlockSpec(memory_space=pltpu.VMEM)] * (len(parts) + len(held)),
            flops=2e8 * blocks,
            name=f"select{blocks}",
        )

    def ffn(own_rows, swapped_rows, after):
        slots = own_rows.shape[0]
        return call(
            ffn_kernel,
            [shape(slots, width)] + [shape(slots, width // SWAPS)] * SWAPS,
            [own_rows, *swapped_rows, gate, up, down],
            after,
            scratch=[pltpu.VMEM((2 * slots, width), BF16)],
            megabytes=24,
            flops=6e7 * slots,
            name=f"ffn{1 + (slots > 100)}",
        )

    def hop(number, high, came, after):
        far_group, near_group = half + 1 - number, half - number
        base = cut if high else 0

        def begins(group, first):
            offset = 0 if group == half else tok_dev
            return (base + first + offset, base + quarter - first)

        groups = [(far_group, begins(far_group, 0))]
        if near_group:
            groups.append((near_group, begins(near_group, quarter)))
        return call(
            functools.partial(hop_kernel, tuple(b for _, b in groups), bool(came)),
            [shape(quarter * len(groups), width)] * 2,
            [array for group, _ in groups for array in outs[group]] + list(came),
            after,
            name="hop",
        )

    def send(pair):
        return [round_ring(pair[0], 1), round_ring(pair[1], -1)]

    picked, outs, parts = {}, {}, {0: own}

    def run_select(k, *after):
        own_rows, info, *other_rows = select(
            parts[k], 1 if k in (0, half) else 2, after, [gate, up, down] if k == 0 else []
        )
        picked[k] = (own_rows, across_cores(other_rows), info)

    def run_ffn(k, *after):
        own_rows, swapped_rows, info = picked[k]
        own_out, *swapped_out = ffn(own_rows, swapped_rows, after)
        outs[k] = (info, own_out, *across_cores(swapped_out))

    def selected(k):
        return picked[k][2]

    def worked(k):
        return outs[k][1]

    run_select(0)
    run_ffn(0)
    ahead, behind = list(own), list(own)
    for k in range(1, half):
        ahead = [round_ring(part, 1) for part in ahead]
        behind = [round_ring(part, -1) for part in behind]
        parts[k] = ahead + behind
        run_select(k, *(picked[k - 1][1] if k > 1 else []))
        if k < half - 1:
            run_ffn(k, worked(k - 1))
    early = (worked(half - 3), *picked[half - 2][1])
    ahead[0], behind[0] = tie(ahead[0], *early), tie(behind[0], *early)
    far = []
    for index in range(2):
        far.append(round_ring(ahead[index][:quarter], 1))
        far.append(round_ring(behind[index][quarter:], -1))
    parts[half] = far
    run_select(half, worked(half - 2))
    run_ffn(half - 1, selected(half))
    run_ffn(half, worked(half - 1))

    low_sums, high_sums, mine, last, kept = (), (), None, (), {}
    for number in range(1, half + 1):
        sums = hop(number, False, low_sums, last)
        last = (sums[0],)
        low_sums = send(sums)
        sums = hop(number, True, high_sums, last)
        last = (sums[0],)
        high_sums = send(sums)
        kept[number] = (low_sums, high_sums)
        if mine is None:
            mine = call(own_kernel, [shape(cut, width, F32)] * 2, [*outs[0], rows], last, name="mine")
            last = (mine[0],)
    received = []
    for index in range(2):
        (up_last, down_last), (up, down) = kept[half][index], kept[half - 1][index]
        total = call(
            final_kernel, [shape(cut, width)], [mine[index], up, up_last, down, down_last], name="final"
        )
        received.append(next_section(total[0]))
    return jnp.concatenate(received, axis=0)[None]


def solution(mesh):
    return jax.shard_map(
        local,
        mesh=mesh,
        in_specs=(
            P("pipe", "expert", None),
            P("pipe", "expert", None),
            P("pipe", None),
            P("pipe", None, None),
            P("pipe", "expert", None, None),
            P("pipe", "expert", None, None),
            P("pipe", "expert", None, None),
        ),
        out_specs=P("pipe", "expert", None),
        check_vma=False,
    )
```

```python
import functools

import jax
import jax.numpy as jnp
from jax import lax
from jax.experimental import pallas as pl
from jax.experimental.pallas import tpu as pltpu
from jax.sharding import PartitionSpec as P

F32, BF16 = jnp.float32, jnp.bfloat16
SWAPS = 1
ROWS_LAST = (((1,), (1,)), ((), ()))


def ring_chips(devices):
    depth = devices // 4
    return [2 * z for z in range(depth)] + [2 * z + 1 for z in reversed(range(depth))]


def ring_pairs(devices, by):
    chips = ring_chips(devices)
    count = len(chips)
    return [
        (2 * chip + core, 2 * chips[(place + by) % count] + core)
        for place, chip in enumerate(chips)
        for core in range(2)
    ]


def round_ring(shard, by):
    return lax.ppermute(shard, "expert", ring_pairs(lax.axis_size("expert"), by))


def across_cores(shards):
    devices = lax.axis_size("expert")
    return [lax.ppermute(s, "expert", [(i, i ^ 1) for i in range(devices)]) for s in shards]


def next_section(shard):
    sections = lax.axis_size("pipe")
    return lax.ppermute(shard, "pipe", [(i, (i + 1) % sections) for i in range(sections)])


def call(kernel, out_shapes, operands, after=(), grid=None, in_specs=None, out_specs=None,
         scratch=(), megabytes=16, flops=0, name=None):
    count = len(operands)

    def body(*refs):
        kernel(*refs[:count], *refs[count + len(after):])

    if in_specs is None:
        in_specs = [pl.BlockSpec(memory_space=pltpu.VMEM)] * count
    if out_specs is None:
        out_specs = [pl.BlockSpec(memory_space=pltpu.VMEM)] * len(out_shapes)
    return pl.pallas_call(
        body,
        name=name,
        out_shape=out_shapes,
        grid=grid or (),
        in_specs=list(in_specs) + [pl.BlockSpec(memory_space=pl.ANY)] * len(after),
        out_specs=out_specs,
        scratch_shapes=list(scratch),
        compiler_params=pltpu.CompilerParams(vmem_limit_bytes=megabytes * 2**20),
        cost_estimate=pl.CostEstimate(flops=int(flops), bytes_accessed=0, transcendentals=0),
    )(*operands, *after)


def prepare_kernel(*refs):
    sources, (low, high), held, arrived = refs[:4], refs[4:6], refs[6:10], refs[10]
    copies = [
        pltpu.make_async_copy(source, target, arrived.at[index])
        for index, (source, target) in enumerate(zip(sources, held))
    ]
    for copy in copies:
        copy.start()
    for copy in copies:
        copy.wait()
    tokens, gain, router, routes = held
    cut, width = low.shape[0], tokens.shape[1]
    experts = router.shape[0]
    wide = tokens[...].astype(F32)
    mean_square = jnp.mean(wide * wide, axis=-1, keepdims=True)
    normed = (wide * lax.rsqrt(mean_square + 1e-06) * gain[...]).astype(BF16)
    low[:, :width] = normed[:cut]
    high[...] = normed[cut:]
    logits = lax.dot_general(router[...], normed, ROWS_LAST, preferred_element_type=F32)
    score = jax.nn.sigmoid(logits)
    ids = lax.broadcasted_iota(jnp.int32, logits.shape, 0)
    named = ids == routes[0]
    for k in range(1, routes.shape[0]):
        named = named | (ids == routes[k])
    total = jnp.sum(jnp.where(named, score, 0.0), axis=0, keepdims=True)
    table = jnp.where(named, (score / total).astype(BF16).astype(F32), -1.0)
    rest = jnp.zeros((cut - experts, logits.shape[1]), F32)
    low[:, width:] = jnp.concatenate([table, rest], axis=0).astype(BF16)


def select_kernel(capacity, blocks, count, names, *refs):
    parts = refs[:count]
    own, info, others = refs[-2 - SWAPS], refs[-1 - SWAPS], refs[-SWAPS:]
    slots, width = own.shape
    tok_dev = parts[0].shape[1] - width
    both = tok_dev * blocks
    firsts = parts[:: len(parts) // blocks]
    table = jnp.concatenate([part[:, width:] for part in firsts], axis=1).astype(F32)
    ids = lax.broadcasted_iota(jnp.int32, table.shape, 0)
    first = jnp.sum(jnp.where(ids == names[0], table, 0.0), axis=0, keepdims=True)
    second = jnp.sum(jnp.where(ids == names[1], table, 0.0), axis=0, keepdims=True)
    line = lax.broadcasted_iota(jnp.int32, (8, both), 0)
    gates = jnp.where(line == 0, first, jnp.where(line == 1, second, -1.0))
    named = gates >= 0
    row = lax.broadcasted_iota(jnp.int32, (both, both), 0)
    column = lax.broadcasted_iota(jnp.int32, (both, both), 1)
    same = (row >= tok_dev) == (column >= tok_dev)
    earlier = jnp.where((row < column) & same, 1.0, 0.0).astype(BF16)
    ranks = jnp.dot(jnp.where(named, 1.0, 0.0).astype(BF16), earlier, preferred_element_type=F32)
    place = lax.broadcasted_iota(jnp.int32, (8, both), 1)
    ranks = jnp.where(place >= tok_dev, ranks + capacity, ranks)
    ranks = jnp.where(named, ranks, -1.0)
    slot = lax.broadcasted_iota(jnp.int32, (slots, both), 0).astype(F32)
    rows = jnp.concatenate([part[:, :width] for part in parts], axis=0)
    hits = [jnp.where(slot == ranks[e : e + 1], 1.0, 0.0).astype(BF16) for e in range(2)]
    taken = jnp.dot(jnp.concatenate(hits, axis=0), rows, preferred_element_type=F32).astype(BF16)
    own[...] = taken[:slots]
    span = width // SWAPS
    for index, other in enumerate(others):
        other[...] = taken[slots:, index * span : (index + 1) * span]
    lines = jnp.where(line < 2, gates, pltpu.roll(ranks, 2, 0))
    spare = jnp.zeros((128 - 8, both), F32)
    info[...] = jnp.concatenate([lines, spare], axis=0).T


def ffn_kernel(own, *refs):
    swapped, (gate, up, down), refs = refs[:SWAPS], refs[SWAPS : SWAPS + 3], refs[SWAPS + 3 :]
    own_out, swapped_outs, rows = refs[0], refs[1 : 1 + SWAPS], refs[1 + SWAPS]
    slots, span = swapped[0].shape
    rows[:slots] = own[...]
    for index, part in enumerate(swapped):
        rows[slots:, index * span : (index + 1) * span] = part[...]

    gate_part = jnp.dot(rows[...], gate[...], preferred_element_type=F32)
    up_part = jnp.dot(rows[...], up[...], preferred_element_type=F32)
    hidden = (gate_part / (1.0 + jnp.exp(-gate_part)) * up_part).astype(BF16)
    result = jnp.dot(hidden, down[...], preferred_element_type=F32)
    own_out[...] = result[:slots].astype(BF16)
    for index, target in enumerate(swapped_outs):
        target[...] = result[slots:, index * span : (index + 1) * span].astype(BF16)


def weights_of(info, begin, count, slots):
    block = info[begin : begin + count, :]
    slot = lax.broadcasted_iota(jnp.int32, (count, slots), 1).astype(F32)
    return [
        jnp.where(slot == block[:, 2 + e : 3 + e], block[:, e : e + 1], 0.0).astype(BF16)
        for e in range(2)
    ]


def expert_sum(begins, count, info, own_out, *other_out):
    slots = own_out.shape[0]
    weights = [weights_of(info, begin, count, slots) for begin in begins]
    own_weights = jnp.concatenate([w[0] for w in weights], axis=0)
    other_weights = jnp.concatenate([w[1] for w in weights], axis=0)
    return jnp.dot(own_weights, own_out[...], preferred_element_type=F32) + jnp.concatenate(
        [jnp.dot(other_weights, o[...], preferred_element_type=F32) for o in other_out], axis=1
    )


def own_kernel(*refs):
    outs, (tokens, low, high) = refs[:-3], refs[-3:]
    cut = low.shape[0]
    value = expert_sum((0,), 2 * cut, *outs) + tokens[...].astype(F32)
    low[...] = value[:cut]
    high[...] = value[cut:]


def tie(array, *tokens):
    return lax.optimization_barrier((array, *tokens))[0]


def final_kernel(mine, up, up_last, down, down_last, target):
    quarter = up_last.shape[0]
    for here, first, second in ((0, up_last, down), (quarter, up, down_last)):
        begin = quarter if first is up else 0
        value = mine[here : here + quarter, :] + first[begin : begin + quarter, :].astype(F32)
        begin = quarter if second is down else 0
        value += second[begin : begin + quarter, :].astype(F32)
        target[here : here + quarter, :] = value.astype(BF16)


def hop_kernel(begins, sums, *refs):
    size = 2 + SWAPS
    count = refs[-1].shape[0] // len(begins)
    came, targets = refs[size * len(begins) : -2], refs[-2:]
    for place, pair in enumerate(begins):
        part = expert_sum(pair, count, *refs[size * place : size * (place + 1)])
        for index, target in enumerate(targets):
            value = part[index * count : (index + 1) * count]
            here = pl.ds(place * count, count)
            if sums:
                value += came[index][here, :].astype(F32)
            target[here, :] = value.astype(target.dtype)


def shape(rows, columns, dtype=BF16):
    return jax.ShapeDtypeStruct((rows, columns), dtype)


def local(tokens, routes, norm_gain, router_weight, w_gate, w_up, w_down):
    rows = tokens[0]
    devices = lax.axis_size("expert")
    chips = devices // 2
    half = chips // 2
    tok_dev, top_count = routes.shape[1:]
    width = rows.shape[1]
    cut, quarter = tok_dev // 2, tok_dev // 4
    capacity = 3 * tok_dev * top_count // (2 * devices)
    device = lax.axis_index("expert")
    names = jnp.stack([device, device ^ 1]).astype(jnp.int32)
    gate, up, down = w_gate[0, 0], w_up[0, 0], w_down[0, 0]

    sources = [rows, norm_gain, router_weight[0].T, jnp.transpose(routes, (2, 0, 1))]
    own = call(
        prepare_kernel,
        [shape(cut, width + tok_dev), shape(cut, width)],
        sources,
        name="prepare",
        in_specs=[pl.BlockSpec(memory_space=pltpu.HBM)] * len(sources),
        scratch=[pltpu.VMEM(a.shape, a.dtype) for a in sources]
        + [pltpu.SemaphoreType.DMA((len(sources),))],
        megabytes=56,
    )

    def select(parts, blocks, after, held=()):
        slots = -(-blocks * capacity // 16) * 16
        return call(
            functools.partial(select_kernel, capacity, blocks, len(parts)),
            [shape(slots, width), shape(blocks * tok_dev, 128, F32)]
            + [shape(slots, width // SWAPS)] * SWAPS,
            [names, *parts, *held],
            after,
            in_specs=[pl.BlockSpec(memory_space=pltpu.SMEM)]
            + [pl.BlockSpec(memory_space=pltpu.VMEM)] * (len(parts) + len(held)),
            flops=2e8 * blocks,
            name=f"select{blocks}",
        )

    def ffn(own_rows, swapped_rows, after):
        slots = own_rows.shape[0]
        return call(
            ffn_kernel,
            [shape(slots, width)] + [shape(slots, width // SWAPS)] * SWAPS,
            [own_rows, *swapped_rows, gate, up, down],
            after,
            scratch=[pltpu.VMEM((2 * slots, width), BF16)],
            megabytes=24,
            flops=6e7 * slots,
            name=f"ffn{1 + (slots > 100)}",
        )

    def hop(number, high, came, after):
        far_group, near_group = half + 1 - number, half - number
        base = cut if high else 0

        def begins(group, first):
            offset = 0 if group == half else tok_dev
            return (base + first + offset, base + quarter - first)

        groups = [(far_group, begins(far_group, 0))]
        if near_group:
            groups.append((near_group, begins(near_group, quarter)))
        return call(
            functools.partial(hop_kernel, tuple(b for _, b in groups), bool(came)),
            [shape(quarter * len(groups), width)] * 2,
            [array for group, _ in groups for array in outs[group]] + list(came),
            after,
            name="hop",
        )

    def send(pair):
        return [round_ring(pair[0], 1), round_ring(pair[1], -1)]

    picked, outs, parts = {}, {}, {0: own}

    def run_select(k, *after):
        own_rows, info, *other_rows = select(
            parts[k], 1 if k in (0, half) else 2, after, [gate, up, down] if k == 0 else []
        )
        picked[k] = (own_rows, across_cores(other_rows), info)

    def run_ffn(k, *after):
        own_rows, swapped_rows, info = picked[k]
        own_out, *swapped_out = ffn(own_rows, swapped_rows, after)
        outs[k] = (info, own_out, *across_cores(swapped_out))

    def selected(k):
        return picked[k][2]

    def worked(k):
        return outs[k][1]

    run_select(0)
    run_ffn(0)
    ahead, behind = list(own), list(own)
    for k in range(1, half):
        ahead = [round_ring(part, 1) for part in ahead]
        behind = [round_ring(part, -1) for part in behind]
        parts[k] = ahead + behind
        run_select(k, *(picked[k - 1][1] if k > 1 else []))
        if k < half - 1:
            run_ffn(k, worked(k - 1))
    early = (worked(half - 3), *picked[half - 2][1])
    ahead[0], behind[0] = tie(ahead[0], *early), tie(behind[0], *early)
    far = []
    for index in range(2):
        far.append(round_ring(ahead[index][:quarter], 1))
        far.append(round_ring(behind[index][quarter:], -1))
    parts[half] = far
    run_select(half, worked(half - 2))
    run_ffn(half - 1, selected(half))
    run_ffn(half, worked(half - 1))

    low_sums, high_sums, mine, last, kept = (), (), None, (), {}
    for number in range(1, half + 1):
        sums = hop(number, False, low_sums, last)
        last = (sums[0],)
        low_sums = send(sums)
        sums = hop(number, True, high_sums, last)
        last = (sums[0],)
        high_sums = send(sums)
        kept[number] = (low_sums, high_sums)
        if mine is None:
            mine = call(own_kernel, [shape(cut, width, F32)] * 2, [*outs[0], rows], last, name="mine")
            last = (mine[0],)
    received = []
    for index in range(2):
        (up_last, down_last), (up, down) = kept[half][index], kept[half - 1][index]
        total = call(
            final_kernel, [shape(cut, width)], [mine[index], up, up_last, down, down_last], name="final"
        )
        received.append(next_section(total[0]))
    return jnp.concatenate(received, axis=0)[None]


def solution(mesh):
    return jax.shard_map(
        local,
        mesh=mesh,
        in_specs=(
            P("pipe", "expert", None),
            P("pipe", "expert", None),
            P("pipe", None),
            P("pipe", None, None),
            P("pipe", "expert", None, None),
            P("pipe", "expert", None, None),
            P("pipe", "expert", None, None),
        ),
        out_specs=P("pipe", "expert", None),
        check_vma=False,
    )
```
